256 devices in a mesh: rep: 16 (over z_lo, y), fsdp: 16 (over x, z_hi, core).
Axes of the slice: x: 4, y: 4, z: 8 (z_hi: 2, z_lo: 4; z = z_hi * 4 + z_lo), core: 2. Of those that a mesh axis runs over, the one named last changes fastest.
Arguments:
- acts: bfloat16 [16, 4096, 2560], P('rep', 'fsdp'), may hold values from -6 to 6
- target: bfloat16 [16, 4096, 2560], P('rep', 'fsdp'), may hold values from -6 to 6
- weight_num: float32 [16, 2560, 2560], P('rep', 'fsdp'), may hold values from -6 to 6
- gain_num: float32 [16, 2560], P('rep'), may hold values from 0.5 to 1.5
- push_weight: float32 [16], P('rep'), may hold values from 0.5 to 2
- step: int32 [1], replicated, may hold values from 0 to 63
Outputs:
- new_weight_num: float32 [16, 2560, 2560], P('rep', 'fsdp')
- new_gain_num: float32 [16, 2560], P('rep')
- new_push_weight: float32 [16], P('rep')
- input_gradient: bfloat16 [16, 4096, 2560], P('rep', 'fsdp')
- loss: float32 [16], P('rep')
The draws below stay inside these ranges and needn't reach their ends.
All inputs are finite; a program needn't handle non-finite values.
Results may differ from the reference program's by a relative error of at most 0.007.
Values may be sent and summed in bfloat16 or wider, within the bound.
No kernel may reach another device: no remote copies, remote signals or barrier semaphores. Data moves between devices by JAX's collectives and lax.ppermute only.
A program may use at most 128 MiB of HBM per device.

```python
import math
import jax
import jax.numpy as jnp
from jax import lax

DM = 2560
DH = 2560
TOK_DEV = 256
TOK_G = 4096
GROUPS = 16
N_REP = 16
N_FSDP = 16


def spiked(drawn, key, source, target, parts, factor):
    def block_of(position):
        return (jnp.arange(drawn.shape[position]) // (drawn.shape[position] // parts)).reshape((-1,) + (1,) * (drawn.ndim - 1 - position))

    near = jax.random.permutation(key, parts)[block_of(target)]
    other_side = (block_of(target) + parts // 2) % parts
    return jnp.where((block_of(source) == near) | (block_of(source) == other_side), factor * drawn, drawn)


def steps_of(rng, shape, cuts, smallest, high):
    def one(dim, blocks):
        steps = jax.random.uniform(jax.random.fold_in(jax.random.fold_in(rng, 6), dim), (blocks,), jnp.float32, smallest / len(cuts), high / len(cuts))
        return jnp.repeat(jnp.exp(steps), shape[dim] // blocks).reshape((-1,) + (1,) * (len(shape) - dim - 1))

    factor_of = one(*cuts[0])
    for cut in cuts[1:]:
        factor_of = factor_of * one(*cut)
    return factor_of


def bell_draw(own_key, shape, scale, reach, shards=(), held_as=jnp.bfloat16):
    level = steps_of(own_key, shape, shards, -0.22, 0.18) if shards else 1.0
    result = jax.random.normal(own_key, shape, jnp.float32) * scale * level
    return jnp.minimum(jnp.maximum(result, -reach), reach).astype(held_as)


def heavy_noise(key, shape, width, most, shards, heavy, kind=jnp.bfloat16):
    result = width * jax.random.normal(key, shape, jnp.float32)
    if shards:
        result = result * steps_of(key, shape, shards, -0.22, 0.18)
    return jnp.clip(spiked(result, jax.random.fold_in(key, 3), *heavy), -most, most).astype(kind)


def setup_inputs(seed: int = 0) -> dict:
    keys = jax.random.split(jax.random.key(seed), 7)
    acts = heavy_noise(keys[0], (GROUPS, TOK_G, DM), 1.0, 6.0, ((0, 16), (1, 16)), (1, 2, 16, 2.0))
    target = bell_draw(keys[1], (GROUPS, TOK_G, DH), 1.0, 6.0, ((0, 16), (1, 16)))
    weight_num = bell_draw(keys[2], (GROUPS, DM, DH), 1.0, 6.0, ((0, 16), (1, 16)), jnp.float32)
    gain_num = jnp.clip(0.5 + 1.0 * jax.random.uniform(keys[3], (GROUPS, DM), jnp.float32) ** steps_of(keys[3], (GROUPS, DM), ((0, 16),), -0.2, 0.2), 0.5, 1.5)
    push_weight = jnp.clip(jnp.exp(math.log(2.0) - 1.3862944 * jax.random.uniform(keys[4], (GROUPS,), jnp.float32) ** steps_of(keys[4], (GROUPS,), ((0, 16),), -0.2, 0.2)), 0.5, 2.0)
    step = jax.random.randint(keys[5], (1,), 0, 64).astype(jnp.int32)
    return {"acts": acts, "target": target, "weight_num": weight_num, "gain_num": gain_num, "push_weight": push_weight, "step": step}


def one_group(items):
    acts_g, target_g, weight_g, gain_g, push_g = items
    scale = DM ** (-0.5)
    token_group = TOK_DEV * N_FSDP
    w_used = (weight_g / push_g).astype(jnp.bfloat16)
    gain_vector = gain_g / push_g
    input_float = acts_g.astype(jnp.float32)
    inverse_norm = lax.rsqrt(lax.optimization_barrier(jnp.mean(input_float * input_float, axis=-1, keepdims=True)) + 1e-05)
    centered_input = input_float * inverse_norm
    normed_rows = (centered_input * gain_vector).astype(jnp.bfloat16)
    out = jnp.dot(normed_rows, w_used, preferred_element_type=jnp.float32) * scale
    diff = out - target_g.astype(jnp.float32)
    loss_g = 0.5 * jnp.sum(diff * diff) / token_group
    d_out = diff.astype(jnp.bfloat16)
    norm_gradient = lax.dot_general(d_out, w_used, (((1,), (1,)), ((), ())), preferred_element_type=jnp.float32) * scale
    scaled_rows = gain_vector * norm_gradient
    input_gradient_group = (inverse_norm * (scaled_rows - centered_input * lax.optimization_barrier(jnp.mean(scaled_rows * centered_input, axis=-1, keepdims=True)))).astype(jnp.bfloat16)
    gain_gradient = lax.optimization_barrier(jnp.sum(norm_gradient * centered_input, axis=0)) * token_group ** (-0.5)
    normed_blocks = normed_rows.reshape(N_FSDP, TOK_DEV, DM)
    dout_blocks = d_out.reshape(N_FSDP, TOK_DEV, DH)

    def add_block(total, block):
        left, right = block
        part = lax.dot_general(left, right, (((0,), (0,)), ((), ())), preferred_element_type=jnp.float32)
        part = lax.optimization_barrier(part.astype(jnp.bfloat16))
        return (total + part.astype(jnp.float32), None)
    summed, unused = lax.scan(add_block, jnp.zeros((DM, DH), jnp.float32), (normed_blocks, dout_blocks))
    weight_grad = summed * (DM * token_group) ** (-0.5)
    weight_half = weight_g - 0.5 * weight_grad
    gain_half = gain_g - 0.05 * gain_gradient
    return (weight_half, gain_half, input_gradient_group, loss_g)

def reference(acts, target, weight_num, gain_num, push_weight, step):
    levels = N_REP.bit_length() - 1
    weight_half, gain_half, input_gradient, loss = lax.map(one_group, (acts, target, weight_num, gain_num, push_weight))
    distance = jnp.power(2, step[0] % levels).astype(jnp.int32)
    new_weight_num = 0.5 * (weight_half + jnp.roll(weight_half, distance, axis=0))
    new_gain_num = 0.5 * (gain_half + jnp.roll(gain_half, distance, axis=0))
    new_push_weight = 0.5 * (push_weight + jnp.roll(push_weight, distance, axis=0))
    return (new_weight_num, new_gain_num, new_push_weight, input_gradient, loss)
```

```python
from functools import partial

import jax
import jax.numpy as jnp
from jax import lax
from jax.experimental import pallas as pl
from jax.experimental.pallas import tpu as pltpu
from jax.sharding import PartitionSpec as P

CHUNKS = (640, 640)
BF16 = jnp.bfloat16
F32 = jnp.float32


def moved(dx=0, swap_z=False, swap_core=False):
    pairs = []
    for i in range(16):
        x, z, c = i // 4, (i // 2) % 2, i % 2
        pairs.append((i, ((x + dx) % 4) * 4 + (z ^ swap_z) * 2 + (c ^ swap_core)))
    return pairs


TO_NEXT, TO_LAST, TO_FAR = moved(dx=1), moved(dx=-1), moved(dx=2)
TO_Z, TO_CORE = moved(swap_z=True), moved(swap_core=True)
TO_PAIR = [(i, i ^ 4) for i in range(16)]


def send(array, pairs):
    return lax.ppermute(array, "fsdp", pairs)


def forward_kernel(scale, info, normed, normed_t, target, *refs):
    w = refs[:8]
    g = refs[8:16]
    d_out, loss, w_v, n_v, t_v, y_v, g_v, d_v, acc, w_sem, n_sem, t_sem, y_sem, g_sem, d_sem = refs[16:]
    x, z = info[0], info[1]
    rows = w[0].shape[0]
    block = 2 * rows

    def part(r):
        return lax.rem(x + r // 2, 4), lax.bitwise_xor(z, r % 2)

    def w_copy(r):
        at = pl.multiple_of(part(r)[1] * rows, rows)
        return pltpu.make_async_copy(w[r], w_v.at[r // 2, pl.ds(at, rows)], w_sem.at[r])

    n_copy = pltpu.make_async_copy(normed, n_v, n_sem)
    t_copy = pltpu.make_async_copy(normed_t, t_v, t_sem)
    y_copy = pltpu.make_async_copy(target, y_v, y_sem)
    n_copy.start()
    for r in range(8):
        w_copy(r).start()
    y_copy.start()
    t_copy.start()
    n_copy.wait()
    for j in range(4):
        w_copy(2 * j).wait()
        w_copy(2 * j + 1).wait()
        at = pl.multiple_of(part(2 * j)[0] * block, block)
        product = jnp.dot(n_v[:, pl.ds(at, block)], w_v[j], preferred_element_type=F32)
        if j:
            acc[...] += product
        else:
            acc[...] = product
    y_copy.wait()
    diff = acc[...] * scale - y_v[...].astype(F32)
    loss[...] = jnp.full(loss.shape, 0.5 * jnp.sum(diff * diff), F32)
    d_v[...] = diff.astype(BF16)
    d_copy = pltpu.make_async_copy(d_v, d_out, d_sem)
    d_copy.start()
    t_copy.wait()
    copies = []
    for r in (5, 4, 3, 7, 2, 6, 1, 0):
        xs, zs = part(r)
        at = pl.multiple_of(xs * block + zs * rows, rows)
        g_v[r] = jnp.dot(t_v[pl.ds(at, rows), :], d_v[...], preferred_element_type=F32).astype(BF16)
        copy = pltpu.make_async_copy(g_v.at[r], g[r], g_sem.at[r])
        copy.start()
        copies.append(copy)
    for copy in copies:
        copy.wait()
    d_copy.wait()


def forward_and_weight_gradient(info, normed, normed_t, target, pieces, scale):
    tokens, depth = normed.shape
    rows, width = pieces[0].shape
    flops = 4 * tokens * depth * width
    any_space = pl.BlockSpec(memory_space=pl.ANY)
    out = pl.pallas_call(
        partial(forward_kernel, scale),
        out_shape=[jax.ShapeDtypeStruct((rows, width), BF16)] * 8
        + [jax.ShapeDtypeStruct((tokens, width), BF16), jax.ShapeDtypeStruct((8, 128), F32)],
        in_specs=[pl.BlockSpec(memory_space=pltpu.SMEM)] + [any_space] * 11,
        out_specs=[any_space] * 9 + [pl.BlockSpec(memory_space=pltpu.VMEM)],
        scratch_shapes=[
            pltpu.VMEM((4, 2 * rows, width), BF16),
            pltpu.VMEM((tokens, depth), BF16),
            pltpu.VMEM((depth, tokens), BF16),
            pltpu.VMEM((tokens, width), BF16),
            pltpu.VMEM((8, rows, width), BF16),
            pltpu.VMEM((tokens, width), BF16),
            pltpu.VMEM((tokens, width), F32),
            pltpu.SemaphoreType.DMA((8,)),
            pltpu.SemaphoreType.DMA,
            pltpu.SemaphoreType.DMA,
            pltpu.SemaphoreType.DMA,
            pltpu.SemaphoreType.DMA((8,)),
            pltpu.SemaphoreType.DMA,
        ],
        compiler_params=pltpu.CompilerParams(vmem_limit_bytes=40 * 2**20),
        cost_estimate=pl.CostEstimate(
            flops=flops, bytes_accessed=4 * tokens * depth + 4 * depth * width, transcendentals=0
        ),
    )(info, normed, normed_t, target, *pieces)
    return out[:8], out[8], out[9]


def backward_kernel(scale, chunks, info, *refs):
    d_out = refs[:chunks]
    w = refs[chunks : 9 * chunks]
    own, other = refs[9 * chunks : 9 * chunks + 2]
    rest = refs[9 * chunks + 2 :]
    d_v, w_v = rest[:chunks], rest[chunks : 2 * chunks]
    o_v, d_sem, w_sem, o_sem = rest[2 * chunks :]
    x, z = info[0], info[1]
    rows = w[0].shape[0]
    block = 2 * rows
    half = own.shape[0]

    def w_copy(k, r):
        at = pl.multiple_of(lax.bitwise_xor(z, r % 2) * rows, rows)
        return pltpu.make_async_copy(
            w[8 * k + r], w_v[k].at[r // 2, pl.ds(at, rows)], w_sem.at[8 * k + r]
        )

    d_copies = [pltpu.make_async_copy(d_out[k], d_v[k], d_sem.at[k]) for k in range(chunks)]
    for copy in d_copies:
        copy.start()
    for r in range(8):
        for k in range(chunks):
            w_copy(k, r).start()
    for copy in d_copies:
        copy.wait()
    out_copies = []
    for j in range(4):
        total = None
        for k in range(chunks):
            w_copy(k, 2 * j).wait()
            w_copy(k, 2 * j + 1).wait()
            product = lax.dot_general(
                d_v[k][...], w_v[k][j], (((1,), (1,)), ((), ())), preferred_element_type=F32
            )
            total = product if total is None else total + product
        o_v[j] = total * scale
        at = pl.multiple_of(lax.rem(x + j, 4) * block, block)
        for i, out in enumerate((own, other)):
            copy = pltpu.make_async_copy(
                o_v.at[j, pl.ds(i * half, half)], out.at[:, pl.ds(at, block)], o_sem.at[2 * j + i]
            )
            copy.start()
            out_copies.append(copy)
    for copy in out_copies:
        copy.wait()


def norm_gradient_parts(info, d_outs, pieces, scale):
    chunks = len(d_outs)
    tokens = d_outs[0].shape[0]
    rows = pieces[0][0].shape[0]
    depth = 8 * rows
    widths = [d.shape[1] for d in d_outs]
    any_space = pl.BlockSpec(memory_space=pl.ANY)
    return pl.pallas_call(
        partial(backward_kernel, scale, chunks),
        out_shape=[jax.ShapeDtypeStruct((tokens // 2, depth), F32)] * 2,
        in_specs=[pl.BlockSpec(memory_space=pltpu.SMEM)] + [any_space] * (9 * chunks),
        out_specs=[any_space] * 2,
        scratch_shapes=[pltpu.VMEM((tokens, width), BF16) for width in widths]
        + [pltpu.VMEM((4, 2 * rows, width), BF16) for width in widths]
        + [
            pltpu.VMEM((4, tokens, 2 * rows), F32),
            pltpu.SemaphoreType.DMA((chunks,)),
            pltpu.SemaphoreType.DMA((8 * chunks,)),
            pltpu.SemaphoreType.DMA((8,)),
        ],
        compiler_params=pltpu.CompilerParams(vmem_limit_bytes=40 * 2**20),
        cost_estimate=pl.CostEstimate(
            flops=2 * tokens * depth * sum(widths),
            bytes_accessed=2 * (tokens + depth) * sum(widths) + 4 * tokens * depth,
            transcendentals=0,
        ),
    )(info, *d_outs, *[piece for of_chunk in pieces for piece in of_chunk])


def total_of(*parts):
    total = parts[0].astype(F32)
    for part in parts[1:]:
        total = total + part.astype(F32)
    return total


def gather(own):
    z = send(own, TO_Z)
    from_last = send(own, TO_NEXT)
    from_next = send(own, TO_LAST)
    from_far = send(from_last, TO_NEXT)
    z_last = send(z, TO_NEXT)
    z_next = send(z, TO_LAST)
    z_far = send(z_next, TO_LAST)
    return [own, z, from_next, z_next, from_far, z_far, from_last, z_last]


def scatter(g):
    far_z = send(g[5], TO_NEXT)
    last_z = send(g[7], TO_LAST)
    next_z = send(total_of(g[3], far_z).astype(BF16), TO_NEXT)
    z = send(total_of(g[1], next_z, last_z).astype(BF16), TO_Z)
    far = send(g[4], TO_LAST)
    following = send(g[2], TO_NEXT)
    last = send(total_of(g[6], far).astype(BF16), TO_LAST)
    return total_of(g[0], following, last, z)


def per_device(acts, target, weight, gain, push, *, distance):
    reps = lax.axis_size("rep")
    to_peer = [(i, (i + distance) % reps) for i in range(reps)]
    index = lax.axis_index("fsdp")
    core = index % 2
    info = jnp.stack([index // 4, (index // 2) % 2]).astype(jnp.int32)
    tokens, depth = acts.shape
    rows, features = weight.shape
    half = features // 2
    token_group = tokens * lax.axis_size("fsdp")
    scale = depth ** (-0.5)

    def columns_of(array, which):
        return lax.dynamic_slice_in_dim(array, which * half, half, axis=1)

    w_used = (weight / push).astype(BF16)
    w_own = columns_of(w_used, core)
    w_core = send(columns_of(w_used, 1 - core), TO_CORE)
    w_rows = jnp.where(
        core == 0,
        jnp.concatenate([w_own, w_core], axis=0),
        jnp.concatenate([w_core, w_own], axis=0),
    )
    acts_both = jnp.concatenate([acts, send(acts, TO_CORE)], axis=0)
    target_both = jnp.concatenate(
        [columns_of(target, core), send(columns_of(target, 1 - core), TO_CORE)], axis=0
    )
    gain_vector = gain / push
    input_float = acts_both.astype(F32)
    inverse_norm = lax.rsqrt(jnp.mean(input_float * input_float, axis=-1, keepdims=True) + 1e-05)
    normed = (input_float * inverse_norm * gain_vector).astype(BF16)
    normed_t = normed.T

    starts = [sum(CHUNKS[:k]) for k in range(len(CHUNKS))]
    pieces, d_outs, losses, sums = [], [], [], []
    for start, width in zip(starts, CHUNKS):
        pieces.append(gather(w_rows[:, start : start + width]))
    for k, (start, width) in enumerate(zip(starts, CHUNKS)):
        g, d_out, loss = forward_and_weight_gradient(
            info, normed, normed_t, target_both[:, start : start + width], pieces[k], scale
        )
        d_outs.append(d_out)
        losses.append(loss[0, 0])
        sums.append(scatter(g))

    norm_own, norm_other = norm_gradient_parts(info, d_outs, pieces, scale)
    norm_gradient = norm_own + send(norm_other, TO_CORE)
    inverse_norm = inverse_norm[:tokens]
    centered = input_float[:tokens] * inverse_norm
    scaled = gain_vector * norm_gradient
    input_gradient = (
        inverse_norm * (scaled - centered * jnp.mean(scaled * centered, axis=-1, keepdims=True))
    ).astype(BF16)
    small = jnp.concatenate(
        [jnp.sum(norm_gradient * centered, axis=0), jnp.broadcast_to(sum(losses), (128,))]
    )[None]
    for pairs in (TO_CORE, TO_Z, TO_PAIR, TO_FAR):
        small = small + send(small, pairs)
    loss = small[0, depth] / token_group
    gain_half = gain - 0.05 * (small[0, :depth] * token_group ** (-0.5))
    state = jnp.concatenate([gain_half, jnp.broadcast_to(push, (128,))])[None]
    new_state = 0.5 * (state + lax.ppermute(state, "rep", to_peer))

    new_parts = ([], [])
    for start, width, total in zip(starts, CHUNKS, sums):
        gradient = total * (depth * token_group) ** (-0.5)
        mine = lax.dynamic_slice_in_dim(gradient, core * rows, rows, axis=0)
        theirs = lax.dynamic_slice_in_dim(gradient, (1 - core) * rows, rows, axis=0)
        back = send(theirs, TO_CORE)
        low = jnp.where(core == 0, mine, back)
        high = jnp.where(core == 0, back, mine)
        weight_half = jnp.concatenate(
            [
                weight[:, start : start + width] - 0.5 * low,
                weight[:, half + start : half + start + width] - 0.5 * high,
            ],
            axis=1,
        )
        peer = lax.ppermute(weight_half.astype(BF16), "rep", to_peer).astype(F32)
        new = 0.5 * (weight_half + peer)
        new_parts[0].append(new[:, :width])
        new_parts[1].append(new[:, width:])
    new_weight = jnp.concatenate(new_parts[0] + new_parts[1], axis=1)
    return new_weight, new_state[0, :depth], new_state[0, depth], input_gradient, loss


def step_of_device(acts, target, weight_num, gain_num, push_weight, step):
    levels = lax.axis_size("rep").bit_length() - 1
    branches = [partial(per_device, distance=1 << level) for level in range(levels)]
    outs = lax.switch(
        step[0] % levels, branches, acts[0], target[0], weight_num[0], gain_num[0], push_weight[0]
    )
    return tuple(out[None] for out in outs)


def solution(mesh):
    return jax.shard_map(
        step_of_device,
        mesh=mesh,
        in_specs=(
            P("rep", "fsdp", None),
            P("rep", "fsdp", None),
            P("rep", "fsdp", None),
            P("rep", None),
            P("rep"),
            P(),
        ),
        out_specs=(
            P("rep", "fsdp", None),
            P("rep", None),
            P("rep"),
            P("rep", "fsdp", None),
            P("rep"),
        ),
        check_vma=False,
    )
```

```python
from functools import partial

import jax
import jax.numpy as jnp
from jax import lax
from jax.experimental import pallas as pl
from jax.experimental.pallas import tpu as pltpu
from jax.sharding import PartitionSpec as P

CHUNKS = (640, 640)
VMEM_BYTES = 56 * 2**20
BF16 = jnp.bfloat16
F32 = jnp.float32


def moved(dx=0, swap_z=False, swap_core=False):
    pairs = []
    for i in range(16):
        x, z, c = i // 4, (i // 2) % 2, i % 2
        pairs.append((i, ((x + dx) % 4) * 4 + (z ^ swap_z) * 2 + (c ^ swap_core)))
    return pairs


TO_NEXT, TO_LAST, TO_FAR = moved(dx=1), moved(dx=-1), moved(dx=2)
TO_Z, TO_CORE = moved(swap_z=True), moved(swap_core=True)
TO_PAIR = [(i, i ^ 4) for i in range(16)]


def send(array, pairs, name):
    with jax.named_scope(name):
        return lax.ppermute(array, "fsdp", pairs)


def tie_kernel(*refs):
    del refs


def after(value, *others):
    any_space = pl.BlockSpec(memory_space=pl.ANY)
    return pl.pallas_call(
        tie_kernel,
        out_shape=jax.ShapeDtypeStruct(value.shape, value.dtype),
        in_specs=[any_space] * (1 + len(others)),
        out_specs=any_space,
        input_output_aliases={0: 0},
        cost_estimate=pl.CostEstimate(flops=0, bytes_accessed=0, transcendentals=0),
    )(value, *others)


def in_vmem(array):
    return array


def vmem_out(shape, dtype):
    return jax.ShapeDtypeStruct(shape, dtype)


def used_kernel(core, inverse, weight, mine, theirs):
    half = mine.shape[1]
    for out, which in ((mine, core[0]), (theirs, 1 - core[0])):
        at = pl.ds(pl.multiple_of(which * half, half), half)
        out[...] = (weight[:, at] * inverse[0]).astype(BF16)


def weights_in_use(core, inverse, weight):
    rows, features = weight.shape
    smem, vmem = pl.BlockSpec(memory_space=pltpu.SMEM), pl.BlockSpec(memory_space=pltpu.VMEM)
    return pl.pallas_call(
        used_kernel,
        out_shape=[vmem_out((rows, features // 2), BF16)] * 2,
        in_specs=[smem, smem, vmem],
        out_specs=[vmem] * 2,
    )(core, inverse, weight)


def rows_kernel(starts, core, mine, theirs, *outs):
    rows = mine.shape[0]
    for start, out in zip(starts, outs):
        columns = slice(start, start + out.shape[1])
        for part, which in ((mine, core[0]), (theirs, 1 - core[0])):
            out[pl.ds(pl.multiple_of(which * rows, rows), rows), :] = part[:, columns]


def rows_of_chip(core, mine, theirs):
    rows = mine.shape[0]
    smem, vmem = pl.BlockSpec(memory_space=pltpu.SMEM), pl.BlockSpec(memory_space=pltpu.VMEM)
    return pl.pallas_call(
        partial(rows_kernel, [0, 0, CHUNKS[0]]),
        out_shape=[vmem_out((2 * rows, width), BF16) for width in (sum(CHUNKS), *CHUNKS)],
        in_specs=[smem, vmem, vmem],
        out_specs=[vmem] * 3,
    )(core, in_vmem(mine), in_vmem(theirs))


def norm_kernel(acts, gain, later, out):
    del later
    tokens = acts[...].astype(F32)
    inverse = lax.rsqrt(jnp.mean(tokens * tokens, axis=-1, keepdims=True) + 1e-05)
    out[...] = (tokens * inverse * gain[...]).astype(BF16)


def normed_tokens(acts, gain, later):
    vmem = pl.BlockSpec(memory_space=pltpu.VMEM)
    return pl.pallas_call(
        norm_kernel,
        out_shape=jax.ShapeDtypeStruct(acts.shape, BF16),
        in_specs=[vmem, vmem, pl.BlockSpec(memory_space=pl.ANY)],
        out_specs=vmem,
    )(acts, gain[None], later)


def column_slices():
    first, second = CHUNKS
    return [(0, first + second), (0, first), (first, second)]


def piece_copies(pieces, whole, sem, x, z, outward=False):
    copies = []
    rows = pieces[0].shape[0]
    for r in range(4):
        for k, (start, width) in enumerate(column_slices()):
            if outward:
                part = whole.at[2 * r + (k > 0), :, pl.ds(start, width)]
                copies.append(pltpu.make_async_copy(part, pieces[3 * r + k], sem.at[3 * r + k]))
                continue
            xs, zs = lax.rem(x + r, 4), lax.bitwise_xor(z, int(k > 0))
            at = pl.multiple_of((2 * xs + zs) * rows, rows)
            part = whole.at[pl.ds(at, rows), pl.ds(start, width)]
            copies.append(pltpu.make_async_copy(pieces[3 * r + k], part, sem.at[3 * r + k]))
    return copies


def wait_for_rows(pieces, whole, sem, x, xs):
    r = lax.rem(xs + 4 - x, 4)
    rows = pieces[0].shape[0]
    for k, (start, width) in enumerate(column_slices()):
        part = whole.at[pl.ds(0, rows), pl.ds(start, width)]
        pltpu.make_async_copy(pieces[k], part, sem.at[3 * r + k]).wait()


def forward_kernel(scale, info, *refs):
    normed, normed_t, targets = refs[:2], refs[2:4], refs[4:6]
    w, g, (d_out, loss) = refs[6:18], refs[18:30], refs[30:32]
    w_v, n_v, t_v, y_v, g_v, d_v, w_sem, n_sem, t_sem, y_sem, g_sem, d_sem = refs[32:]
    x, z, core = info[0], info[1], info[2]
    rows, width = w[0].shape
    tokens, depth = normed[0].shape
    half = depth // 2
    own = pl.multiple_of(core * width, width)

    w_copies = piece_copies(w, w_v, w_sem, x, z)
    n_copies = [
        [
            pltpu.make_async_copy(
                normed[i].at[:, pl.ds(h * half, half)],
                n_v.at[i, :, pl.ds(h * half, half)],
                n_sem.at[2 * h + i],
            )
            for i in range(2)
        ]
        for h in range(2)
    ]
    y_copies = [
        pltpu.make_async_copy(targets[0].at[:, pl.ds(own, width)], y_v.at[0], y_sem.at[0]),
        pltpu.make_async_copy(targets[1], y_v.at[1], y_sem.at[1]),
    ]
    t_copies = [pltpu.make_async_copy(normed_t[i], t_v.at[i], t_sem.at[i]) for i in range(2)]
    for copy in n_copies[0] + w_copies + n_copies[1] + y_copies + t_copies:
        copy.start()
    outs = [None, None]
    for h in range(2):
        for copy in n_copies[h]:
            copy.wait()
        for xs in range(2 * h, 2 * h + 2):
            wait_for_rows(w, w_v, w_sem, x, xs)
        for i in range(2):
            product = jnp.dot(
                n_v[i, :, h * half : (h + 1) * half],
                w_v[h * half : (h + 1) * half, :],
                preferred_element_type=F32,
            )
            outs[i] = outs[i] + product if h else product
    total = 0.0
    for i in range(2):
        y_copies[i].wait()
        diff = outs[i] * scale - y_v[i].astype(F32)
        total += 0.5 * jnp.sum(diff * diff)
        d_v[i * tokens : (i + 1) * tokens, :] = diff.astype(BF16)
    loss[...] = jnp.full(loss.shape, total, F32)
    d_copy = pltpu.make_async_copy(d_v, d_out, d_sem)
    d_copy.start()
    for copy in t_copies:
        copy.wait()
    g_copies = piece_copies(g, g_v, g_sem, x, z, outward=True)
    for r in (2, 1, 3, 0):
        for row, ks in ((1, (1, 2)), (0, (0,))):
            xs, zs = lax.rem(x + r, 4), lax.bitwise_xor(z, row)
            at = pl.ds(pl.multiple_of((2 * xs + zs) * rows, rows), rows)
            product = jnp.dot(t_v[0, at, :], d_v[:tokens, :], preferred_element_type=F32)
            product += jnp.dot(t_v[1, at, :], d_v[tokens:, :], preferred_element_type=F32)
            g_v[2 * r + row] = product.astype(BF16)
            for k in ks:
                g_copies[3 * r + k].start()
    for copy in g_copies:
        copy.wait()
    d_copy.wait()


def forward_and_weight_gradient(info, normed, normed_t, targets, pieces, scale):
    tokens, depth = normed[0].shape
    rows, width = pieces[0].shape
    any_space = pl.BlockSpec(memory_space=pl.ANY)
    out = pl.pallas_call(
        partial(forward_kernel, scale),
        out_shape=[jax.ShapeDtypeStruct(piece.shape, BF16) for piece in pieces]
        + [jax.ShapeDtypeStruct((2 * tokens, width), BF16), jax.ShapeDtypeStruct((8, 128), F32)],
        in_specs=[pl.BlockSpec(memory_space=pltpu.SMEM)] + [any_space] * 18,
        out_specs=[any_space] * 13 + [pl.BlockSpec(memory_space=pltpu.VMEM)],
        scratch_shapes=[
            pltpu.VMEM((depth, width), BF16),
            pltpu.VMEM((2, tokens, depth), BF16),
            pltpu.VMEM((2, depth, tokens), BF16),
            pltpu.VMEM((2, tokens, width), BF16),
            pltpu.VMEM((8, rows, width), BF16),
            pltpu.VMEM((2 * tokens, width), BF16),
            pltpu.SemaphoreType.DMA((12,)),
            pltpu.SemaphoreType.DMA((4,)),
            pltpu.SemaphoreType.DMA((2,)),
            pltpu.SemaphoreType.DMA((2,)),
            pltpu.SemaphoreType.DMA((12,)),
            pltpu.SemaphoreType.DMA,
        ],
        compiler_params=pltpu.CompilerParams(vmem_limit_bytes=VMEM_BYTES),
        cost_estimate=pl.CostEstimate(flops=0, bytes_accessed=0, transcendentals=0),
    )(info, *normed, *normed_t, *targets, *pieces)
    return out[:12], out[12], out[13]


def backward_kernel(scale, extra, info, *refs):
    refs = refs[extra:]
    d_out, w, outs = refs[0], refs[1:13], refs[13:15]
    d_v, w_v, own_v, other_v, d_sem, w_sem, o_sem = refs[15:]
    x, z = info[0], info[1]
    tokens, depth = outs[0].shape
    half = depth // 2
    d_copy = pltpu.make_async_copy(d_out, d_v, d_sem)
    d_copy.start()
    for copy in piece_copies(w, w_v, w_sem, x, z):
        copy.start()
    d_copy.wait()
    out_copies = []
    for h in range(2):
        for xs in range(2 * h, 2 * h + 2):
            wait_for_rows(w, w_v, w_sem, x, xs)
        product = scale * lax.dot_general(
            d_v[...],
            w_v[h * half : (h + 1) * half, :],
            (((1,), (1,)), ((), ())),
            preferred_element_type=F32,
        )
        for i, held in enumerate((own_v, other_v)):
            held[h] = product[i * tokens : (i + 1) * tokens].astype(held.dtype)
            copy = pltpu.make_async_copy(
                held.at[h], outs[i].at[:, pl.ds(h * half, half)], o_sem.at[2 * h + i]
            )
            copy.start()
            out_copies.append(copy)
    for copy in out_copies:
        copy.wait()


def norm_gradient_parts(info, d_out, pieces, scale, deps=()):
    tokens = d_out.shape[0] // 2
    rows, width = pieces[0].shape
    depth = 8 * rows
    any_space = pl.BlockSpec(memory_space=pl.ANY)
    return pl.pallas_call(
        partial(backward_kernel, scale, len(deps)),
        out_shape=[
            jax.ShapeDtypeStruct((tokens, depth), F32),
            jax.ShapeDtypeStruct((tokens, depth), BF16),
        ],
        in_specs=[pl.BlockSpec(memory_space=pltpu.SMEM)] + [any_space] * (13 + len(deps)),
        out_specs=[any_space] * 2,
        scratch_shapes=[
            pltpu.VMEM((2 * tokens, width), BF16),
            pltpu.VMEM((depth, width), BF16),
            pltpu.VMEM((2, tokens, depth // 2), F32),
            pltpu.VMEM((2, tokens, depth // 2), BF16),
            pltpu.SemaphoreType.DMA,
            pltpu.SemaphoreType.DMA((12,)),
            pltpu.SemaphoreType.DMA((4,)),
        ],
        compiler_params=pltpu.CompilerParams(vmem_limit_bytes=VMEM_BYTES),
        cost_estimate=pl.CostEstimate(flops=0, bytes_accessed=0, transcendentals=0),
    )(info, *deps, d_out, *pieces)


def total_kernel(rows, start, scale, extra, core, *refs):
    parts, (mine, theirs) = refs[extra:-2], refs[-2:]
    width = mine.shape[1]
    for out, which in ((mine, core[0]), (theirs, 1 - core[0])):
        at = pl.ds(pl.multiple_of(which * rows, rows), rows)
        total = 0.0
        for part in parts:
            first = 0 if part.shape[1] == width else start
            total += part[at, first : first + width].astype(F32)
        out[...] = total * scale


def total_by_core(core, parts, start, width, scale, deps=()):
    rows = parts[0].shape[0] // 2
    vmem = pl.BlockSpec(memory_space=pltpu.VMEM)
    return pl.pallas_call(
        partial(total_kernel, rows, start, scale, len(deps)),
        out_shape=[vmem_out((rows, width), F32)] * 2,
        in_specs=[pl.BlockSpec(memory_space=pltpu.SMEM)]
        + [pl.BlockSpec(memory_space=pl.ANY)] * len(deps)
        + [vmem] * len(parts),
        out_specs=[vmem] * 2,
        cost_estimate=pl.CostEstimate(flops=0, bytes_accessed=0, transcendentals=0),
    )(core, *deps, *map(in_vmem, parts))


def total_of(*parts):
    total = parts[0].astype(F32)
    for part in parts[1:]:
        total = total + part.astype(F32)
    return total


def per_device(acts, target, weight, gain, push, step):
    reps = lax.axis_size("rep")
    index = lax.axis_index("fsdp")
    core = index % 2
    info = jnp.stack([index // 4, (index // 2) % 2, core]).astype(jnp.int32)
    tokens, depth = acts.shape
    rows, features = weight.shape
    half = features // 2
    token_group = tokens * lax.axis_size("fsdp")
    scale = depth ** (-0.5)
    starts = [sum(CHUNKS[:k]) for k in range(len(CHUNKS))]

    def exchange(parts):
        def branch(distance, parts):
            pairs = [(i, (i + distance) % reps) for i in range(reps)]
            return [lax.ppermute(part, "rep", pairs) for part in parts]

        levels = reps.bit_length() - 1
        branches = [partial(branch, 1 << level) for level in range(levels)]
        return lax.switch(step % levels, branches, parts)

    which_core = core.astype(jnp.int32)[None]
    w_mine, w_theirs = weights_in_use(which_core, (1.0 / push)[None], weight)
    own, own_a, own_b = rows_of_chip(which_core, w_mine, send(w_theirs, TO_CORE, "w_core"))

    last = send(own, TO_NEXT, "last")
    z_a = send(own_a, TO_Z, "z_a")
    next_ = send(own, TO_LAST, "next")
    z_b = send(own_b, TO_Z, "z_b")
    far = send(last, TO_NEXT, "far")
    z_a = after(z_a, next_, last)
    z_next_a = send(z_a, TO_LAST, "z_next_a")
    z_last_a = send(z_a, TO_NEXT, "z_last_a")
    z_far_a = send(z_next_a, TO_LAST, "z_far_a")
    z_b = after(z_b, far, z_far_a)
    z_next_b = send(z_b, TO_LAST, "z_next_b")
    z_last_b = send(z_b, TO_NEXT, "z_last_b")
    z_far_b = send(z_next_b, TO_LAST, "z_far_b")
    pieces = [
        *(own, z_a, z_b),
        *(next_, z_next_a, z_next_b),
        *(far, z_far_a, z_far_b),
        *(last, z_last_a, z_last_b),
    ]

    gain_vector = gain / push
    input_float = acts.astype(F32)
    inverse_norm = lax.rsqrt(jnp.mean(input_float * input_float, axis=-1, keepdims=True) + 1e-05)
    normed_own = normed_tokens(acts, gain_vector, w_theirs)
    normed = (normed_own, send(normed_own, TO_CORE, "normed"))
    normed_t = (normed[0].T, normed[1].T)
    target_theirs = lax.dynamic_slice_in_dim(target, (1 - core) * half, half, axis=1)
    targets = (target, send(target_theirs, TO_CORE, "target"))

    g, d_out, loss_part = forward_and_weight_gradient(
        info, normed, normed_t, targets, pieces, scale
    )

    r_far_a = send(g[7], TO_NEXT, "r_far_a")
    r_last_a = send(g[10], TO_LAST, "r_last_a")
    r_far_b = send(g[8], TO_NEXT, "r_far_b")
    r_last_b = send(g[11], TO_LAST, "r_last_b")
    r_far = send(g[6], TO_LAST, "r_far")
    norm_own, norm_other = norm_gradient_parts(info, d_out, pieces, scale)
    r_next_a = send(total_of(g[4], r_far_a).astype(BF16), TO_NEXT, "r_next_a")
    r_next_b = send(total_of(g[5], r_far_b).astype(BF16), TO_NEXT, "r_next_b")
    r_next = send(after(g[3], r_next_b), TO_NEXT, "r_next")
    r_z_a = send(total_of(g[1], r_next_a, r_last_a).astype(BF16), TO_Z, "r_z_a")
    r_last = send(total_of(g[9], r_far).astype(BF16), TO_LAST, "r_last")
    r_z_b = send(total_of(g[2], r_next_b, r_last_b).astype(BF16), TO_Z, "r_z_b")
    norm_core = send(norm_other, TO_CORE, "norm_core")

    norm_gradient = norm_own + norm_core.astype(F32)
    centered = input_float * inverse_norm
    scaled = gain_vector * norm_gradient
    input_gradient = (
        inverse_norm * (scaled - centered * jnp.mean(scaled * centered, axis=-1, keepdims=True))
    ).astype(BF16)
    losses = loss_part[0, 0]
    small = jnp.concatenate(
        [jnp.sum(norm_gradient * centered, axis=0), jnp.broadcast_to(losses, (128,))]
    )[None]
    for name, pairs in (("core", TO_CORE), ("z", TO_Z), ("pair", TO_PAIR), ("far", TO_FAR)):
        before_last = small
        small = small + send(small, pairs, "sum_" + name)
    loss = small[0, depth] / token_group
    gain_half = gain - 0.05 * (small[0, :depth] * token_group ** (-0.5))
    state = jnp.concatenate([gain_half, jnp.broadcast_to(push, (128,))])[None]

    weight_scale = (depth * token_group) ** (-0.5)

    def updated(k, parts, deps):
        start, width = starts[k], CHUNKS[k]
        mine, theirs = total_by_core(which_core, parts, start, width, weight_scale, deps)
        back = send(theirs, TO_CORE, "r_core%d" % k)
        low = jnp.where(core == 0, mine, back)
        high = jnp.where(core == 0, back, mine)
        return jnp.concatenate(
            [
                weight[:, start : start + width] - 0.5 * low,
                weight[:, half + start : half + start + width] - 0.5 * high,
            ],
            axis=1,
        )

    weight0 = updated(0, (g[0], r_next, r_last, r_z_a), ())
    (peer0,) = exchange([weight0.astype(BF16)])
    weight1 = updated(1, (g[0], r_next, r_last, r_z_b), (peer0, before_last))
    peer1, peer_state = exchange([weight1.astype(BF16), state])
    new_state = 0.5 * (state + peer_state)
    new0 = 0.5 * (weight0 + peer0.astype(F32))
    new1 = 0.5 * (weight1 + peer1.astype(F32))
    n0, n1 = CHUNKS
    new_weight = jnp.concatenate([new0[:, :n0], new1[:, :n1], new0[:, n0:], new1[:, n1:]], axis=1)
    return new_weight, new_state[0, :depth], new_state[0, depth], input_gradient, loss


def step_of_device(acts, target, weight_num, gain_num, push_weight, step):
    outs = per_device(acts[0], target[0], weight_num[0], gain_num[0], push_weight[0], step[0])
    return tuple(out[None] for out in outs)


def solution(mesh):
    return jax.shard_map(
        step_of_device,
        mesh=mesh,
        in_specs=(
            P("rep", "fsdp", None),
            P("rep", "fsdp", None),
            P("rep", "fsdp", None),
            P("rep", None),
            P("rep"),
            P(),
        ),
        out_specs=(
            P("rep", "fsdp", None),
            P("rep", None),
            P("rep"),
            P("rep", "fsdp", None),
            P("rep"),
        ),
        check_vma=False,
    )
```

```python
from functools import partial

import jax
import jax.numpy as jnp
from jax import lax
from jax.experimental import pallas as pl
from jax.experimental.pallas import tpu as pltpu
from jax.sharding import PartitionSpec as P

CHUNKS = (640, 640)
VMEM_BYTES = 56 * 2**20
BF16 = jnp.bfloat16
F32 = jnp.float32


def moved(dx=0, swap_z=False, swap_core=False):
    pairs = []
    for i in range(16):
        x, z, c = i // 4, (i // 2) % 2, i % 2
        pairs.append((i, ((x + dx) % 4) * 4 + (z ^ swap_z) * 2 + (c ^ swap_core)))
    return pairs


TO_NEXT, TO_LAST, TO_FAR = moved(dx=1), moved(dx=-1), moved(dx=2)
TO_Z, TO_CORE = moved(swap_z=True), moved(swap_core=True)
TO_PAIR = [(i, i ^ 4) for i in range(16)]


def send(array, pairs, name):
    with jax.named_scope(name):
        return lax.ppermute(array, "fsdp", pairs)


def tie_kernel(*refs):
    del refs


def after(value, *others):
    any_space = pl.BlockSpec(memory_space=pl.ANY)
    return pl.pallas_call(
        tie_kernel,
        out_shape=jax.ShapeDtypeStruct(value.shape, value.dtype),
        in_specs=[any_space] * (1 + len(others)),
        out_specs=any_space,
        input_output_aliases={0: 0},
        cost_estimate=pl.CostEstimate(flops=0, bytes_accessed=0, transcendentals=0),
    )(value, *others)


def in_vmem(array):
    return array


def vmem_out(shape, dtype):
    return jax.ShapeDtypeStruct(shape, dtype)


def used_kernel(core, inverse, weight, mine, theirs):
    half = mine.shape[1]
    for out, which in ((mine, core[0]), (theirs, 1 - core[0])):
        at = pl.ds(pl.multiple_of(which * half, half), half)
        out[...] = (weight[:, at] * inverse[0]).astype(BF16)


def weights_in_use(core, inverse, weight):
    rows, features = weight.shape
    smem, vmem = pl.BlockSpec(memory_space=pltpu.SMEM), pl.BlockSpec(memory_space=pltpu.VMEM)
    return pl.pallas_call(
        used_kernel,
        out_shape=[vmem_out((rows, features // 2), BF16)] * 2,
        in_specs=[smem, smem, vmem],
        out_specs=[vmem] * 2,
    )(core, inverse, weight)


def rows_kernel(starts, core, mine, theirs, *outs):
    rows = mine.shape[0]
    for start, out in zip(starts, outs):
        columns = slice(start, start + out.shape[1])
        for part, which in ((mine, core[0]), (theirs, 1 - core[0])):
            out[pl.ds(pl.multiple_of(which * rows, rows), rows), :] = part[:, columns]


def rows_of_chip(core, mine, theirs):
    rows = mine.shape[0]
    smem, vmem = pl.BlockSpec(memory_space=pltpu.SMEM), pl.BlockSpec(memory_space=pltpu.VMEM)
    return pl.pallas_call(
        partial(rows_kernel, [0, 0, CHUNKS[0]]),
        out_shape=[vmem_out((2 * rows, width), BF16) for width in (sum(CHUNKS), *CHUNKS)],
        in_specs=[smem, vmem, vmem],
        out_specs=[vmem] * 3,
    )(core, in_vmem(mine), in_vmem(theirs))


def norm_kernel(acts, gain, later, out):
    del later
    tokens = acts[...].astype(F32)
    inverse = lax.rsqrt(jnp.mean(tokens * tokens, axis=-1, keepdims=True) + 1e-05)
    out[...] = (tokens * inverse * gain[...]).astype(BF16)


def normed_tokens(acts, gain, later):
    vmem = pl.BlockSpec(memory_space=pltpu.VMEM)
    return pl.pallas_call(
        norm_kernel,
        out_shape=jax.ShapeDtypeStruct(acts.shape, BF16),
        in_specs=[vmem, vmem, pl.BlockSpec(memory_space=pl.ANY)],
        out_specs=vmem,
    )(acts, gain[None], later)


def column_slices():
    first, second = CHUNKS
    return [(0, first + second), (0, first), (first, second)]


def piece_copies(pieces, whole, sem, x, z, outward=False):
    copies = []
    rows = pieces[0].shape[0]
    for r in range(4):
        for k, (start, width) in enumerate(column_slices()):
            if outward:
                part = whole.at[2 * r + (k > 0), :, pl.ds(start, width)]
                copies.append(pltpu.make_async_copy(part, pieces[3 * r + k], sem.at[3 * r + k]))
                continue
            xs, zs = lax.rem(x + r, 4), lax.bitwise_xor(z, int(k > 0))
            at = pl.multiple_of((2 * xs + zs) * rows, rows)
            part = whole.at[pl.ds(at, rows), pl.ds(start, width)]
            copies.append(pltpu.make_async_copy(pieces[3 * r + k], part, sem.at[3 * r + k]))
    return copies


def wait_for_rows(pieces, whole, sem, x, xs):
    r = lax.rem(xs + 4 - x, 4)
    rows = pieces[0].shape[0]
    for k, (start, width) in enumerate(column_slices()):
        part = whole.at[pl.ds(0, rows), pl.ds(start, width)]
        pltpu.make_async_copy(pieces[k], part, sem.at[3 * r + k]).wait()


def forward_kernel(scale, info, *refs):
    normed, normed_t, targets = refs[:2], refs[2:4], refs[4:6]
    w, g, (d_out, loss) = refs[6:18], refs[18:30], refs[30:32]
    w_v, n_v, t_v, y_v, g_v, d_v, w_sem, n_sem, t_sem, y_sem, g_sem, d_sem = refs[32:]
    x, z, core = info[0], info[1], info[2]
    rows, width = w[0].shape
    tokens, depth = normed[0].shape
    half = depth // 2
    own = pl.multiple_of(core * width, width)

    w_copies = piece_copies(w, w_v, w_sem, x, z)
    n_copies = [
        [
            pltpu.make_async_copy(
                normed[i].at[:, pl.ds(h * half, half)],
                n_v.at[i, :, pl.ds(h * half, half)],
                n_sem.at[2 * h + i],
            )
            for i in range(2)
        ]
        for h in range(2)
    ]
    y_copies = [
        pltpu.make_async_copy(targets[0].at[:, pl.ds(own, width)], y_v.at[0], y_sem.at[0]),
        pltpu.make_async_copy(targets[1], y_v.at[1], y_sem.at[1]),
    ]
    t_copies = [pltpu.make_async_copy(normed_t[i], t_v.at[i], t_sem.at[i]) for i in range(2)]
    for copy in n_copies[0] + w_copies + n_copies[1] + y_copies + t_copies:
        copy.start()
    outs = [None, None]
    for h in range(2):
        for copy in n_copies[h]:
            copy.wait()
        for xs in range(2 * h, 2 * h + 2):
            wait_for_rows(w, w_v, w_sem, x, xs)
        for i in range(2):
            product = jnp.dot(
                n_v[i, :, h * half : (h + 1) * half],
                w_v[h * half : (h + 1) * half, :],
                preferred_element_type=F32,
            )
            outs[i] = outs[i] + product if h else product
    total = 0.0
    for i in range(2):
        y_copies[i].wait()
        diff = outs[i] * scale - y_v[i].astype(F32)
        total += 0.5 * jnp.sum(diff * diff)
        d_v[i * tokens : (i + 1) * tokens, :] = diff.astype(BF16)
    loss[...] = jnp.full(loss.shape, total, F32)
    d_copy = pltpu.make_async_copy(d_v, d_out, d_sem)
    d_copy.start()
    for copy in t_copies:
        copy.wait()
    g_copies = piece_copies(g, g_v, g_sem, x, z, outward=True)
    for r in (2, 1, 3, 0):
        for row, ks in ((1, (1, 2)), (0, (0,))):
            xs, zs = lax.rem(x + r, 4), lax.bitwise_xor(z, row)
            at = pl.ds(pl.multiple_of((2 * xs + zs) * rows, rows), rows)
            product = jnp.dot(t_v[0, at, :], d_v[:tokens, :], preferred_element_type=F32)
            product += jnp.dot(t_v[1, at, :], d_v[tokens:, :], preferred_element_type=F32)
            g_v[2 * r + row] = product.astype(BF16)
            for k in ks:
                g_copies[3 * r + k].start()
    for copy in g_copies:
        copy.wait()
    d_copy.wait()


def forward_and_weight_gradient(info, normed, normed_t, targets, pieces, scale):
    tokens, depth = normed[0].shape
    rows, width = pieces[0].shape
    any_space = pl.BlockSpec(memory_space=pl.ANY)
    out = pl.pallas_call(
        partial(forward_kernel, scale),
        out_shape=[jax.ShapeDtypeStruct(piece.shape, BF16) for piece in pieces]
        + [jax.ShapeDtypeStruct((2 * tokens, width), BF16), jax.ShapeDtypeStruct((8, 128), F32)],
        in_specs=[pl.BlockSpec(memory_space=pltpu.SMEM)] + [any_space] * 18,
        out_specs=[any_space] * 13 + [pl.BlockSpec(memory_space=pltpu.VMEM)],
        scratch_shapes=[
            pltpu.VMEM((depth, width), BF16),
            pltpu.VMEM((2, tokens, depth), BF16),
            pltpu.VMEM((2, depth, tokens), BF16),
            pltpu.VMEM((2, tokens, width), BF16),
            pltpu.VMEM((8, rows, width), BF16),
            pltpu.VMEM((2 * tokens, width), BF16),
            pltpu.SemaphoreType.DMA((12,)),
            pltpu.SemaphoreType.DMA((4,)),
            pltpu.SemaphoreType.DMA((2,)),
            pltpu.SemaphoreType.DMA((2,)),
            pltpu.SemaphoreType.DMA((12,)),
            pltpu.SemaphoreType.DMA,
        ],
        compiler_params=pltpu.CompilerParams(vmem_limit_bytes=VMEM_BYTES),
        cost_estimate=pl.CostEstimate(flops=0, bytes_accessed=0, transcendentals=0),
    )(info, *normed, *normed_t, *targets, *pieces)
    return out[:12], out[12], out[13]


def backward_kernel(scale, extra, info, *refs):
    refs = refs[extra:]
    d_out, w, outs = refs[0], refs[1:13], refs[13:15]
    d_v, w_v, own_v, other_v, d_sem, w_sem, o_sem = refs[15:]
    x, z = info[0], info[1]
    tokens, depth = outs[0].shape
    half = depth // 2
    d_copy = pltpu.make_async_copy(d_out, d_v, d_sem)
    d_copy.start()
    for copy in piece_copies(w, w_v, w_sem, x, z):
        copy.start()
    d_copy.wait()
    out_copies = []
    for h in range(2):
        for xs in range(2 * h, 2 * h + 2):
            wait_for_rows(w, w_v, w_sem, x, xs)
        product = scale * lax.dot_general(
            d_v[...],
            w_v[h * half : (h + 1) * half, :],
            (((1,), (1,)), ((), ())),
            preferred_element_type=F32,
        )
        for i, held in enumerate((own_v, other_v)):
            held[h] = product[i * tokens : (i + 1) * tokens].astype(held.dtype)
            copy = pltpu.make_async_copy(
                held.at[h], outs[i].at[:, pl.ds(h * half, half)], o_sem.at[2 * h + i]
            )
            copy.start()
            out_copies.append(copy)
    for copy in out_copies:
        copy.wait()


def norm_gradient_parts(info, d_out, pieces, scale, deps=()):
    tokens = d_out.shape[0] // 2
    rows, width = pieces[0].shape
    depth = 8 * rows
    any_space = pl.BlockSpec(memory_space=pl.ANY)
    return pl.pallas_call(
        partial(backward_kernel, scale, len(deps)),
        out_shape=[
            jax.ShapeDtypeStruct((tokens, depth), F32),
            jax.ShapeDtypeStruct((tokens, depth), BF16),
        ],
        in_specs=[pl.BlockSpec(memory_space=pltpu.SMEM)] + [any_space] * (13 + len(deps)),
        out_specs=[any_space] * 2,
        scratch_shapes=[
            pltpu.VMEM((2 * tokens, width), BF16),
            pltpu.VMEM((depth, width), BF16),
            pltpu.VMEM((2, tokens, depth // 2), F32),
            pltpu.VMEM((2, tokens, depth // 2), BF16),
            pltpu.SemaphoreType.DMA,
            pltpu.SemaphoreType.DMA((12,)),
            pltpu.SemaphoreType.DMA((4,)),
        ],
        compiler_params=pltpu.CompilerParams(vmem_limit_bytes=VMEM_BYTES),
        cost_estimate=pl.CostEstimate(flops=0, bytes_accessed=0, transcendentals=0),
    )(info, *deps, d_out, *pieces)


def total_kernel(rows, start, scale, extra, core, *refs):
    parts, (mine, theirs) = refs[extra:-2], refs[-2:]
    width = mine.shape[1]
    for out, which in ((mine, core[0]), (theirs, 1 - core[0])):
        at = pl.ds(pl.multiple_of(which * rows, rows), rows)
        total = 0.0
        for part in parts:
            first = 0 if part.shape[1] == width else start
            total += part[at, first : first + width].astype(F32)
        out[...] = total * scale


def total_by_core(core, parts, start, width, scale, deps=()):
    rows = parts[0].shape[0] // 2
    vmem = pl.BlockSpec(memory_space=pltpu.VMEM)
    return pl.pallas_call(
        partial(total_kernel, rows, start, scale, len(deps)),
        out_shape=[vmem_out((rows, width), F32)] * 2,
        in_specs=[pl.BlockSpec(memory_space=pltpu.SMEM)]
        + [pl.BlockSpec(memory_space=pl.ANY)] * len(deps)
        + [vmem] * len(parts),
        out_specs=[vmem] * 2,
        cost_estimate=pl.CostEstimate(flops=0, bytes_accessed=0, transcendentals=0),
    )(core, *deps, *map(in_vmem, parts))


def total_of(*parts):
    total = parts[0].astype(F32)
    for part in parts[1:]:
        total = total + part.astype(F32)
    return total


def per_device(acts, target, weight, gain, push, step):
    reps = lax.axis_size("rep")
    index = lax.axis_index("fsdp")
    core = index % 2
    info = jnp.stack([index // 4, (index // 2) % 2, core]).astype(jnp.int32)
    tokens, depth = acts.shape
    rows, features = weight.shape
    half = features // 2
    token_group = tokens * lax.axis_size("fsdp")
    scale = depth ** (-0.5)
    starts = [sum(CHUNKS[:k]) for k in range(len(CHUNKS))]

    def exchange(parts):
        def branch(distance, parts):
            pairs = [(i, (i + distance) % reps) for i in range(reps)]
            return [lax.ppermute(part, "rep", pairs) for part in parts]

        levels = reps.bit_length() - 1
        branches = [partial(branch, 1 << level) for level in range(levels)]
        return lax.switch(step % levels, branches, parts)

    which_core = core.astype(jnp.int32)[None]
    w_mine, w_theirs = weights_in_use(which_core, (1.0 / push)[None], weight)
    own, own_a, own_b = rows_of_chip(which_core, w_mine, send(w_theirs, TO_CORE, "w_core"))

    last = send(own, TO_NEXT, "last")
    z_a = send(own_a, TO_Z, "z_a")
    next_ = send(own, TO_LAST, "next")
    z_b = send(own_b, TO_Z, "z_b")
    far = send(last, TO_NEXT, "far")
    z_a = after(z_a, next_, last)
    z_next_a = send(z_a, TO_LAST, "z_next_a")
    z_last_a = send(z_a, TO_NEXT, "z_last_a")
    z_far_a = send(z_next_a, TO_LAST, "z_far_a")
    z_b = after(z_b, far, z_far_a)
    z_next_b = send(z_b, TO_LAST, "z_next_b")
    z_last_b = send(z_b, TO_NEXT, "z_last_b")
    z_far_b = send(z_next_b, TO_LAST, "z_far_b")
    pieces = [
        *(own, z_a, z_b),
        *(next_, z_next_a, z_next_b),
        *(far, z_far_a, z_far_b),
        *(last, z_last_a, z_last_b),
    ]

    gain_vector = gain / push
    input_float = acts.astype(F32)
    inverse_norm = lax.rsqrt(jnp.mean(input_float * input_float, axis=-1, keepdims=True) + 1e-05)
    normed_own = normed_tokens(acts, gain_vector, w_theirs)
    normed = (normed_own, send(normed_own, TO_CORE, "normed"))
    normed_t = (normed[0].T, normed[1].T)
    target_theirs = lax.dynamic_slice_in_dim(target, (1 - core) * half, half, axis=1)
    targets = (target, send(target_theirs, TO_CORE, "target"))

    g, d_out, loss_part = forward_and_weight_gradient(
        info, normed, normed_t, targets, pieces, scale
    )

    r_far_a = send(g[7], TO_NEXT, "r_far_a")
    r_last_a = send(g[10], TO_LAST, "r_last_a")
    r_far_b = send(g[8], TO_NEXT, "r_far_b")
    r_last_b = send(g[11], TO_LAST, "r_last_b")
    r_far = send(g[6], TO_LAST, "r_far")
    norm_own, norm_other = norm_gradient_parts(info, d_out, pieces, scale)
    r_next_a = send(total_of(g[4], r_far_a).astype(BF16), TO_NEXT, "r_next_a")
    r_next_b = send(total_of(g[5], r_far_b).astype(BF16), TO_NEXT, "r_next_b")
    r_next = send(after(g[3], r_next_b), TO_NEXT, "r_next")
    r_z_a = send(total_of(g[1], r_next_a, r_last_a).astype(BF16), TO_Z, "r_z_a")
    r_last = send(total_of(g[9], r_far).astype(BF16), TO_LAST, "r_last")
    r_z_b = send(total_of(g[2], r_next_b, r_last_b).astype(BF16), TO_Z, "r_z_b")
    norm_core = send(after(norm_other, r_far_b, r_last_a), TO_CORE, "norm_core")

    norm_gradient = norm_own + norm_core.astype(F32)
    centered = input_float * inverse_norm
    scaled = gain_vector * norm_gradient
    input_gradient = (
        inverse_norm * (scaled - centered * jnp.mean(scaled * centered, axis=-1, keepdims=True))
    ).astype(BF16)
    losses = loss_part[0, 0]
    small = jnp.concatenate(
        [jnp.sum(norm_gradient * centered, axis=0), jnp.broadcast_to(losses, (128,))]
    )[None]
    for name, pairs in (("core", TO_CORE), ("z", TO_Z), ("pair", TO_PAIR), ("far", TO_FAR)):
        before_last = small
        small = small + send(small, pairs, "sum_" + name)
    loss = small[0, depth] / token_group
    gain_half = gain - 0.05 * (small[0, :depth] * token_group ** (-0.5))
    state = jnp.concatenate([gain_half, jnp.broadcast_to(push, (128,))])[None]

    weight_scale = (depth * token_group) ** (-0.5)

    def updated(k, parts, deps):
        start, width = starts[k], CHUNKS[k]
        mine, theirs = total_by_core(which_core, parts, start, width, weight_scale, deps)
        back = send(theirs, TO_CORE, "r_core%d" % k)
        low = jnp.where(core == 0, mine, back)
        high = jnp.where(core == 0, back, mine)
        return jnp.concatenate(
            [
                weight[:, start : start + width] - 0.5 * low,
                weight[:, half + start : half + start + width] - 0.5 * high,
            ],
            axis=1,
        )

    weight0 = updated(0, (g[0], r_next, r_last, r_z_a), ())
    (peer0,) = exchange([weight0.astype(BF16)])
    weight1 = updated(1, (g[0], r_next, r_last, r_z_b), (peer0, before_last))
    peer1, peer_state = exchange([weight1.astype(BF16), state])
    new_state = 0.5 * (state + peer_state)
    new0 = 0.5 * (weight0 + peer0.astype(F32))
    new1 = 0.5 * (weight1 + peer1.astype(F32))
    n0, n1 = CHUNKS
    new_weight = jnp.concatenate([new0[:, :n0], new1[:, :n1], new0[:, n0:], new1[:, n1:]], axis=1)
    return new_weight, new_state[0, :depth], new_state[0, depth], input_gradient, loss


def step_of_device(acts, target, weight_num, gain_num, push_weight, step):
    outs = per_device(acts[0], target[0], weight_num[0], gain_num[0], push_weight[0], step[0])
    return tuple(out[None] for out in outs)


def solution(mesh):
    return jax.shard_map(
        step_of_device,
        mesh=mesh,
        in_specs=(
            P("rep", "fsdp", None),
            P("rep", "fsdp", None),
            P("rep", "fsdp", None),
            P("rep", None),
            P("rep"),
            P(),
        ),
        out_specs=(
            P("rep", "fsdp", None),
            P("rep", None),
            P("rep"),
            P("rep", "fsdp", None),
            P("rep"),
        ),
        check_vma=False,
    )
```
